1024 devices in a mesh: ep: 64 (over z, core), fsdp: 16 (over x, y).
Axes of the slice: x: 4, y: 4, z: 32, core: 2. Of those that a mesh axis runs over, the one named last changes fastest.
Arguments:
- tokens: bfloat16 [8192, 3072], P(('ep', 'fsdp')), may hold values from -6 to 6
- out_grad: bfloat16 [8192, 3072], P(('ep', 'fsdp')), may hold values from -6 to 6
- routes: int32 [8192, 2], P(('ep', 'fsdp')), may hold values from 0 to 7, as said below
- probs: bfloat16 [8192, 2], P(('ep', 'fsdp')), may hold values from 0.099609375 to 1
- gate_elems: bfloat16 [3072, 8192], P('fsdp', 'ep'), may hold values from -0.109375 to 0.109375
- gate_scales: bfloat16 [96, 8192], P('fsdp', 'ep'), may hold values from 0.5 to 2
- up_elems: bfloat16 [3072, 8192], P('fsdp', 'ep'), may hold values from -0.109375 to 0.109375
- up_scales: bfloat16 [96, 8192], P('fsdp', 'ep'), may hold values from 0.5 to 2
- down_elems: bfloat16 [8192, 3072], P('ep', 'fsdp'), may hold values from -0.0625 to 0.0625
- down_scales: bfloat16 [8192, 96], P('ep', 'fsdp'), may hold values from 0.5 to 2
Outputs:
- input_grad: bfloat16 [8192, 3072], P(('ep', 'fsdp'))
- prob_grad: float32 [8192], P(('ep', 'fsdp'))
- gate_grad: float32 [3072, 8192], P('fsdp', 'ep')
- up_grad: float32 [3072, 8192], P('fsdp', 'ep')
- down_grad: float32 [8192, 3072], P('ep', 'fsdp')
The draws below stay inside these ranges and needn't reach their ends.
Inputs may be any that keep to these rules, and one draw needn't show every extreme that they name: `routes`: each token names 2 different experts. Among the 8 tokens of one device, between 1 and 2 name expert 0, and some device has exactly 2.
All inputs are finite; a program needn't handle non-finite values.
Results may differ from the reference program's by a relative error of at most 0.015.
Values may be sent and summed in bfloat16 or wider, within the bound.
No kernel may reach another device: no remote copies, remote signals or barrier semaphores. Data moves between devices by JAX's collectives and lax.ppermute only.
A program may use at most 32 MiB of HBM per device.

```python
import math
import jax
import jax.numpy as jnp
from jax import lax

D = 3072
FFW = 8192
EXPERTS = 8
TOP = 2
BLOCK = 32
CAP = 2
TOK_DEV = 8
TOKENS = 8192
N_EP = 64
N_FSDP = 16


def permute_block(subkey):
    return jax.random.permutation(subkey, TOK_DEV)


def draw_routes(key, part):
    key = jax.random.fold_in(key, 7)
    keys = jax.random.split(key, 6)
    blocks = TOKENS // TOK_DEV
    counts = jax.random.randint(keys[0], (blocks,), 1, CAP + 1)
    fullest = jax.random.randint(keys[1], (), 0, blocks)
    counts = jnp.where(jnp.arange(blocks) == fullest, CAP, counts)
    ranks = jax.vmap(permute_block)(jax.random.split(keys[2], blocks))
    picked = ranks < counts[:, None]
    first = jax.random.randint(keys[3], (blocks, TOK_DEV), 1, EXPERTS)
    offset = jax.random.randint(keys[4], (blocks, TOK_DEV), 1, EXPERTS - 1)
    second = 1 + (first - 1 + offset) % (EXPERTS - 1)
    place = jax.random.randint(keys[5], (blocks, TOK_DEV), 0, 2)
    first = jnp.where(jnp.logical_and(picked, place == 0), 0, first)
    second = jnp.where(jnp.logical_and(picked, place == 1), 0, second)
    return jnp.stack([first, second], axis=-1).reshape(TOKENS, TOP).astype(jnp.int32)


def shard_levels(rng, shape, cuts, least, largest):
    loudness, own = 1.0, jax.random.fold_in(rng, 6)
    for axis_at, parts in cuts:
        heights = jnp.exp(jax.random.uniform(jax.random.fold_in(own, axis_at), (parts,), jnp.float32, least / len(cuts), largest / len(cuts)))
        loudness = loudness * jnp.repeat(heights, shape[axis_at] // parts).reshape([-1 if axis == axis_at else 1 for axis in range(len(shape))])
    return loudness


def centred(key, dims, deviation, most, cuts=(), kind=jnp.bfloat16):
    level = shard_levels(key, dims, cuts, -0.22, 0.18) if cuts else 1.0
    result = jax.random.normal(key, dims, jnp.float32) * deviation * level
    return jnp.minimum(jnp.maximum(result, -most), most).astype(kind)


def setup_inputs(seed: int = 0) -> dict:
    arg_keys = jax.random.split(jax.random.key(seed), 11)
    return {
        "tokens": centred(arg_keys[0], (TOKENS, D), 1.0, 6.0, ((0, 1024),)),
        "out_grad": centred(arg_keys[1], (TOKENS, D), 1.0, 6.0, ((0, 1024),)),
        "routes": draw_routes(jax.random.fold_in(arg_keys[10], 71), 0),
        "probs": jnp.clip(0.099609375 + 0.9003906 * jax.random.uniform(arg_keys[3], (TOKENS, TOP), jnp.float32) ** shard_levels(arg_keys[3], (TOKENS, TOP), ((0, 1024),), -0.2, 0.2), 0.099609375, 1.0).astype(jnp.bfloat16),
        "gate_elems": centred(arg_keys[4], (D, FFW), D ** -0.5, 0.109375, ((0, 16), (1, 64))),
        "gate_scales": jnp.clip(jnp.exp(math.log(2.0) - 1.3862944 * jax.random.uniform(arg_keys[5], (D // BLOCK, FFW), jnp.float32) ** shard_levels(arg_keys[5], (D // BLOCK, FFW), ((0, 16), (1, 64)), -0.2, 0.2)), 0.5, 2.0).astype(jnp.bfloat16),
        "up_elems": centred(arg_keys[6], (D, FFW), D ** -0.5, 0.109375, ((0, 16), (1, 64))),
        "up_scales": jnp.clip(jnp.exp(math.log(2.0) - 1.3862944 * jax.random.uniform(arg_keys[7], (D // BLOCK, FFW), jnp.float32) ** shard_levels(arg_keys[7], (D // BLOCK, FFW), ((0, 16), (1, 64)), -0.2, 0.2)), 0.5, 2.0).astype(jnp.bfloat16),
        "down_elems": centred(arg_keys[8], (FFW, D), FFW ** -0.5, 0.0625, ((0, 64), (1, 16))),
        "down_scales": jnp.clip(jnp.exp(math.log(2.0) - 1.3862944 * jax.random.uniform(arg_keys[9], (FFW, D // BLOCK), jnp.float32) ** shard_levels(arg_keys[9], (FFW, D // BLOCK), ((0, 64), (1, 16)), -0.2, 0.2)), 0.5, 2.0).astype(jnp.bfloat16),
    }


def dequantize(elements, scales, along):
    wide = jnp.repeat(scales.astype(jnp.float32), BLOCK, axis=along)
    return (elements.astype(jnp.float32) * wide).astype(jnp.bfloat16)


def column_work(w_gate, w_up, w_down, rows, grads_rows, weights_rows):
    gate_pre = jnp.dot(rows, w_gate, preferred_element_type=jnp.float32)
    lift_pre = jnp.dot(rows, w_up, preferred_element_type=jnp.float32)
    sigmoid_gate = jax.nn.sigmoid(gate_pre)
    activated = gate_pre * sigmoid_gate
    hidden = (activated * lift_pre).astype(jnp.bfloat16)
    scaled_hidden = (weights_rows[:, None] * activated * lift_pre).astype(jnp.bfloat16)
    back = lax.dot_general(grads_rows, w_down, (((1,), (1,)), ((), ())), preferred_element_type=jnp.float32)
    prob_part = jnp.sum(hidden.astype(jnp.float32) * back, axis=1)
    hidden_grad = weights_rows[:, None] * back
    lift_grad = (hidden_grad * activated).astype(jnp.bfloat16)
    gate_pre_grad = (hidden_grad * lift_pre * sigmoid_gate * (1.0 + gate_pre * (1.0 - sigmoid_gate))).astype(jnp.bfloat16)
    input_part = lax.dot_general(gate_pre_grad, w_gate, (((1,), (1,)), ((), ())), preferred_element_type=jnp.float32)
    input_part = input_part + lax.dot_general(lift_grad, w_up, (((1,), (1,)), ((), ())), preferred_element_type=jnp.float32)
    grad_gate = lax.dot_general(rows, gate_pre_grad, (((0,), (0,)), ((), ())), preferred_element_type=jnp.float32)
    grad_up = lax.dot_general(rows, lift_grad, (((0,), (0,)), ((), ())), preferred_element_type=jnp.float32)
    grad_down = lax.dot_general(scaled_hidden, grads_rows, (((0,), (0,)), ((), ())), preferred_element_type=jnp.float32)
    return input_part, prob_part, grad_gate, grad_up, grad_down


def reference(tokens, out_grad, routes, probs, gate_elems, gate_scales, up_elems, up_scales, down_elems, down_scales):
    w_gate = dequantize(gate_elems, gate_scales, 0)
    w_up = dequantize(up_elems, up_scales, 0)
    w_down = dequantize(down_elems, down_scales, 1)
    blocks = TOKENS // TOK_DEV
    first = routes[:, 0] == 0
    second = routes[:, 1] == 0
    chosen = jnp.logical_or(first, second)
    weight = jnp.where(first, probs[:, 0], jnp.where(second, probs[:, 1], jnp.zeros_like(probs[:, 0]))).astype(jnp.float32)
    chosen_blocks = chosen.reshape(blocks, TOK_DEV)
    slot = jnp.cumsum(chosen_blocks.astype(jnp.int32), axis=1) - 1
    slot_ids = jnp.arange(CAP, dtype=jnp.int32)
    select = jnp.logical_and(slot[:, None, :] == slot_ids[None, :, None], chosen_blocks[:, None, :]).astype(jnp.float32)
    tok_blocks = tokens.reshape(blocks, TOK_DEV, D).astype(jnp.float32)
    grad_blocks = out_grad.reshape(blocks, TOK_DEV, D).astype(jnp.float32)
    rows = jnp.einsum('bct,btd->bcd', select, tok_blocks).astype(jnp.bfloat16)
    grads_rows = jnp.einsum('bct,btd->bcd', select, grad_blocks).astype(jnp.bfloat16)
    weights_rows = jnp.einsum('bct,bt->bc', select, weight.reshape(blocks, TOK_DEV))

    def by_column(layout):
        shaped = layout.reshape((N_EP, N_FSDP) + layout.shape[1:])
        shaped = jnp.moveaxis(shaped, 1, 0)
        return shaped.reshape((N_FSDP, N_EP * CAP) + layout.shape[2:])

    col_rows = by_column(rows)
    col_grads = by_column(grads_rows)
    col_weights = by_column(weights_rows)

    def step_fn(carry, inputs):
        input_part, prob_part, grad_gate, grad_up, grad_down = column_work(w_gate, w_up, w_down, inputs[0], inputs[1], inputs[2])
        total_gate = carry[0] + grad_gate.astype(jnp.bfloat16).astype(jnp.float32)
        total_up = carry[1] + grad_up.astype(jnp.bfloat16).astype(jnp.float32)
        total_down = carry[2] + grad_down.astype(jnp.bfloat16).astype(jnp.float32)
        return (total_gate, total_up, total_down), (input_part, prob_part)

    start = (jnp.zeros((D, FFW), jnp.float32), jnp.zeros((D, FFW), jnp.float32), jnp.zeros((FFW, D), jnp.float32))
    totals, outputs = lax.scan(step_fn, start, (col_rows, col_grads, col_weights))
    input_rows = outputs[0].reshape(N_FSDP, N_EP, CAP, D)
    input_rows = jnp.moveaxis(input_rows, 0, 1).reshape(blocks, CAP, D)
    prob_rows = outputs[1].reshape(N_FSDP, N_EP, CAP)
    prob_rows = jnp.moveaxis(prob_rows, 0, 1).reshape(blocks, CAP)
    input_grad = jnp.einsum('bct,bcd->btd', select, input_rows).reshape(TOKENS, D).astype(jnp.bfloat16)
    prob_grad = jnp.einsum('bct,bc->bt', select, prob_rows).reshape(TOKENS)
    return input_grad, prob_grad, totals[0], totals[1], totals[2]
```

```python
import jax
import jax.numpy as jnp
from jax import lax
from jax.sharding import Mesh, PartitionSpec as P

BLOCK = 32
CAP = 2
FAR, NEAR, CORES = 8, 4, 2
X, Y = 4, 4
N_FSDP = X * Y
BF16 = jnp.bfloat16
F32 = jnp.float32


def dequantize(elements, scales):
    groups = elements.shape[0] // BLOCK
    wide = elements.reshape(groups, BLOCK, -1).astype(F32)
    return (wide * scales.astype(F32)[:, None, :]).astype(BF16).reshape(elements.shape)


def local(
    tokens,
    out_grad,
    routes,
    probs,
    gate_elems,
    gate_scales,
    up_elems,
    up_scales,
    down_elems,
    down_scales,
):
    width = tokens.shape[1]
    first = routes[:, 0] == 0
    second = routes[:, 1] == 0
    chosen = jnp.logical_or(first, second)
    weight = jnp.where(
        first, probs[:, 0], jnp.where(second, probs[:, 1], jnp.zeros_like(probs[:, 0]))
    )
    slot = jnp.cumsum(chosen.astype(jnp.int32)) - 1
    slot_ids = jnp.arange(CAP, dtype=jnp.int32)
    select_mask = jnp.logical_and(slot[None, :] == slot_ids[:, None], chosen[None, :])
    select = select_mask.astype(BF16)
    wide_weight = jnp.broadcast_to(weight[:, None], (weight.shape[0], 128))
    both = jnp.concatenate([tokens, out_grad, wide_weight], axis=1)
    payload = jnp.dot(select, both, preferred_element_type=F32).astype(BF16)

    own = jnp.concatenate(
        [
            dequantize(gate_elems, gate_scales),
            dequantize(up_elems, up_scales),
            dequantize(down_elems.T, down_scales.T),
        ],
        axis=1,
    )
    everyone = jnp.broadcast_to(own[None], (N_FSDP,) + own.shape)
    everyone, payload = lax.optimization_barrier((everyone, payload))
    weights = lax.all_to_all(everyone, ("x", "y"), 0, 0, tiled=True)

    along_z = lax.all_gather(payload[None], ("far", "near"), axis=0, tiled=True)
    along_z = along_z.reshape(FAR * NEAR * CAP, payload.shape[1])
    along_z, weights = lax.optimization_barrier((along_z, weights))
    pair = jnp.broadcast_to(along_z[None], (CORES,) + along_z.shape)
    pair = lax.all_to_all(pair, "core", 0, 0, tiled=True)
    all_rows = pair.reshape(CORES * FAR * NEAR * CAP, payload.shape[1])
    rows = all_rows[:, :width]
    grads_rows = all_rows[:, width : 2 * width]
    row_weights = all_rows[:, 2 * width : 2 * width + 1].astype(F32)

    weights = weights.reshape(N_FSDP * own.shape[0], own.shape[1])
    units = gate_elems.shape[1]
    w_gate, w_up, w_down = (
        weights[:, :units],
        weights[:, units : 2 * units],
        weights[:, 2 * units :],
    )

    gate_pre = jnp.dot(rows, w_gate, preferred_element_type=F32)
    lift_pre = jnp.dot(rows, w_up, preferred_element_type=F32)
    back = jnp.dot(grads_rows, w_down, preferred_element_type=F32)
    sigmoid_gate = jax.nn.sigmoid(gate_pre)
    activated = gate_pre * sigmoid_gate
    hidden = (activated * lift_pre).astype(BF16)
    scaled_hidden = (row_weights * activated * lift_pre).astype(BF16)
    prob_part = jnp.sum(hidden.astype(F32) * back, axis=1, keepdims=True)
    hidden_grad = row_weights * back
    lift_grad = (hidden_grad * activated).astype(BF16)
    gate_pre_grad = (
        hidden_grad * lift_pre * sigmoid_gate * (1.0 + gate_pre * (1.0 - sigmoid_gate))
    ).astype(BF16)

    def over_rows(a, b):
        return lax.dot_general(a, b, (((0,), (0,)), ((), ())), preferred_element_type=F32)

    terms = jnp.concatenate(
        [
            over_rows(rows, gate_pre_grad),
            over_rows(rows, lift_grad),
            over_rows(grads_rows, scaled_hidden),
        ],
        axis=1,
    ).astype(BF16)
    terms = terms.reshape((N_FSDP,) + own.shape)
    input_part = lax.dot_general(
        jnp.concatenate([gate_pre_grad, lift_grad], axis=1),
        weights[:, : 2 * units],
        (((1,), (1,)), ((), ())),
        preferred_element_type=F32,
    )

    def pack(values, prob):
        high = prob.astype(BF16)
        low = (prob - high.astype(F32)).astype(BF16)
        pad = jnp.zeros(prob.shape[:-1] + (126,), BF16)
        return jnp.concatenate([values.astype(BF16), high, low, pad], axis=-1)

    def unpack(blocks):
        total = jnp.sum(blocks.astype(F32), axis=0)
        prob = total[..., width : width + 1] + total[..., width + 1 : width + 2]
        return total[..., :width], prob

    part = pack(input_part, prob_part).reshape(CORES, FAR * NEAR * CAP, -1)
    part = lax.all_to_all(part, "core", 0, 0, tiled=True)
    part = pack(*unpack(part)).reshape(FAR, NEAR, CAP, -1)
    part = jnp.swapaxes(part, 0, 1).reshape(NEAR, FAR * CAP, -1)
    part = lax.all_to_all(part, "near", 0, 0, tiled=True)
    part = pack(*unpack(part))
    part, terms = lax.optimization_barrier((part, terms))
    shares = lax.all_to_all(terms, ("x", "y"), 0, 0, tiled=True)
    share = jnp.sum(shares.astype(F32), axis=0)
    part = lax.all_gather(part[None], "far", axis=0, tiled=True)
    mine = CAP * lax.axis_index("far")
    input_rows, prob_rows = unpack(lax.dynamic_slice_in_dim(part, mine, CAP, axis=1))

    mask_float = select_mask.astype(F32)
    input_grad = jnp.sum(
        mask_float[:, :, None] * input_rows.astype(BF16).astype(F32)[:, None, :], axis=0
    ).astype(BF16)
    prob_grad = jnp.sum(mask_float * prob_rows, axis=0)
    gate_grad = share[:, :units]
    up_grad = share[:, units : 2 * units]
    down_grad = share[:, 2 * units :].T
    return (input_grad, prob_grad, gate_grad, up_grad, down_grad)


def solution(mesh):
    fine = Mesh(
        mesh.devices.reshape(FAR, NEAR, CORES, X, Y), ("far", "near", "core", "x", "y")
    )
    ep, fsdp = ("far", "near", "core"), ("x", "y")
    by_token = P(ep + fsdp, None)
    tall, wide = P(fsdp, ep), P(ep, fsdp)
    in_specs = (by_token,) * 4 + (tall,) * 4 + (wide,) * 2
    out_specs = (by_token, P(ep + fsdp), tall, tall, wide)
    return jax.shard_map(
        local, mesh=fine, in_specs=in_specs, out_specs=out_specs, check_vma=False
    )
```

```python
import jax
import jax.numpy as jnp
from jax import lax
from jax.sharding import Mesh, PartitionSpec as P

BLOCK = 32
CAP = 2
FAR, NEAR, CORES = 8, 4, 2
FAR_AXES, NEAR_AXES = ("za", "zb"), ("zc", "zd")
SWAP = [(0, 1), (1, 0)]
X, Y = 4, 4
N_FSDP = X * Y
BF16 = jnp.bfloat16
F32 = jnp.float32


def dequantize(elements, scales):
    groups = elements.shape[0] // BLOCK
    wide = elements.reshape(groups, BLOCK, -1).astype(F32)
    return (wide * scales.astype(F32)[:, None, :]).astype(BF16).reshape(elements.shape)


def local(
    tokens,
    out_grad,
    routes,
    probs,
    gate_elems,
    gate_scales,
    up_elems,
    up_scales,
    down_elems,
    down_scales,
):
    width = tokens.shape[1]
    first = routes[:, 0] == 0
    second = routes[:, 1] == 0
    chosen = jnp.logical_or(first, second)
    weight = jnp.where(
        first, probs[:, 0], jnp.where(second, probs[:, 1], jnp.zeros_like(probs[:, 0]))
    )
    slot = jnp.cumsum(chosen.astype(jnp.int32)) - 1
    slot_ids = jnp.arange(CAP, dtype=jnp.int32)
    select_mask = jnp.logical_and(slot[None, :] == slot_ids[:, None], chosen[None, :])
    select = select_mask.astype(BF16)
    wide_weight = jnp.broadcast_to(weight[:, None], (weight.shape[0], 128))
    both = jnp.concatenate([tokens, out_grad, wide_weight], axis=1)
    payload = jnp.dot(select, both, preferred_element_type=F32).astype(BF16)

    own = jnp.concatenate(
        [
            dequantize(gate_elems, gate_scales),
            dequantize(up_elems, up_scales),
            dequantize(down_elems.T, down_scales.T),
        ],
        axis=1,
    )
    everyone = jnp.broadcast_to(own[None], (N_FSDP,) + own.shape)
    everyone, payload = lax.optimization_barrier((everyone, payload))
    weights = lax.all_to_all(everyone, ("x", "y"), 0, 0, tiled=True)

    along_z = lax.all_gather(payload[None], FAR_AXES, axis=0, tiled=True)
    along_z = along_z.reshape(FAR * CAP, payload.shape[1])
    along_z = lax.all_gather(along_z, NEAR_AXES, axis=0, tiled=True)
    along_z, weights = lax.optimization_barrier((along_z, weights))
    pair = jnp.broadcast_to(along_z[None], (CORES,) + along_z.shape)
    pair = lax.all_to_all(pair, "core", 0, 0, tiled=True)
    all_rows = pair.reshape(CORES * FAR * NEAR * CAP, payload.shape[1])
    rows = all_rows[:, :width]
    grads_rows = all_rows[:, width : 2 * width]
    row_weights = all_rows[:, 2 * width : 2 * width + 1].astype(F32)

    weights = weights.reshape(N_FSDP * own.shape[0], own.shape[1])
    units = gate_elems.shape[1]
    w_gate, w_up, w_down = (
        weights[:, :units],
        weights[:, units : 2 * units],
        weights[:, 2 * units :],
    )

    gate_pre = jnp.dot(rows, w_gate, preferred_element_type=F32)
    lift_pre = jnp.dot(rows, w_up, preferred_element_type=F32)
    back = jnp.dot(grads_rows, w_down, preferred_element_type=F32)
    sigmoid_gate = jax.nn.sigmoid(gate_pre)
    activated = gate_pre * sigmoid_gate
    hidden = (activated * lift_pre).astype(BF16)
    scaled_hidden = (row_weights * activated * lift_pre).astype(BF16)
    prob_part = jnp.sum(hidden.astype(F32) * back, axis=1, keepdims=True)
    hidden_grad = row_weights * back
    lift_grad = (hidden_grad * activated).astype(BF16)
    gate_pre_grad = (
        hidden_grad * lift_pre * sigmoid_gate * (1.0 + gate_pre * (1.0 - sigmoid_gate))
    ).astype(BF16)

    def over_rows(a, b):
        return lax.dot_general(a, b, (((0,), (0,)), ((), ())), preferred_element_type=F32)

    terms = jnp.concatenate(
        [
            over_rows(rows, gate_pre_grad),
            over_rows(rows, lift_grad),
            over_rows(grads_rows, scaled_hidden),
        ],
        axis=1,
    ).astype(BF16)
    terms = terms.reshape((N_FSDP,) + own.shape)
    input_part = lax.dot_general(
        jnp.concatenate([gate_pre_grad, lift_grad], axis=1),
        weights[:, : 2 * units],
        (((1,), (1,)), ((), ())),
        preferred_element_type=F32,
    )

    def pack(values, prob):
        high = prob.astype(BF16)
        low = (prob - high.astype(F32)).astype(BF16)
        pad = jnp.zeros(prob.shape[:-1] + (126,), BF16)
        return jnp.concatenate([values.astype(BF16), high, low, pad], axis=-1)

    def unpack(blocks):
        total = jnp.sum(blocks.astype(F32), axis=0)
        prob = total[..., width : width + 1] + total[..., width + 1 : width + 2]
        return total[..., :width], prob

    part = pack(input_part, prob_part).reshape(CORES, FAR * NEAR * CAP, -1)
    part = lax.all_to_all(part, "core", 0, 0, tiled=True)
    part = pack(*unpack(part)).reshape(NEAR, FAR * CAP, -1)
    part = lax.all_to_all(part, NEAR_AXES, 0, 0, tiled=True)
    part = pack(*unpack(part))
    part, terms = lax.optimization_barrier((part, terms))
    shares = lax.all_to_all(terms, ("x", "y"), 0, 0, tiled=True)
    share = jnp.sum(shares.astype(F32), axis=0)

    def halve(part, axis, where):
        bit = lax.axis_index(axis)
        keep = lax.dynamic_index_in_dim(part, bit, where, keepdims=False)
        give = lax.dynamic_index_in_dim(part, 1 - bit, where, keepdims=False)
        return pack(*unpack(jnp.stack([keep, lax.ppermute(give, axis, SWAP)])))

    part = halve(part.reshape(4, 2, CAP, -1), "zb", 1).reshape(4 * CAP, -1)
    part = lax.all_gather(part[None], "za", axis=0, tiled=True)
    mine = CAP * lax.axis_index("za")
    input_rows, prob_rows = unpack(lax.dynamic_slice_in_dim(part, mine, CAP, axis=1))

    mask_float = select_mask.astype(F32)
    input_grad = jnp.sum(
        mask_float[:, :, None] * input_rows.astype(BF16).astype(F32)[:, None, :], axis=0
    ).astype(BF16)
    prob_grad = jnp.sum(mask_float * prob_rows, axis=0)
    gate_grad = share[:, :units]
    up_grad = share[:, units : 2 * units]
    down_grad = share[:, 2 * units :].T
    return (input_grad, prob_grad, gate_grad, up_grad, down_grad)


def solution(mesh):
    fine = Mesh(
        mesh.devices.reshape(4, 2, 2, 2, CORES, X, Y),
        FAR_AXES + NEAR_AXES + ("core", "x", "y"),
    )
    ep, fsdp = FAR_AXES + NEAR_AXES + ("core",), ("x", "y")
    by_token = P(ep + fsdp, None)
    tall, wide = P(fsdp, ep), P(ep, fsdp)
    in_specs = (by_token,) * 4 + (tall,) * 4 + (wide,) * 2
    out_specs = (by_token, P(ep + fsdp), tall, tall, wide)
    return jax.shard_map(
        local, mesh=fine, in_specs=in_specs, out_specs=out_specs, check_vma=False
    )
```

```python
import jax
import jax.numpy as jnp
from jax import lax
from jax.experimental import pallas as pl
from jax.experimental.pallas import tpu as pltpu
from jax.sharding import Mesh, PartitionSpec as P

BLOCK = 32
CAP = 2
FAR, NEAR, CORES = 8, 4, 2
FAR_AXES, NEAR_AXES = ("za", "zb"), ("zc", "zd")
SWAP = [(0, 1), (1, 0)]
X, Y = 4, 4
N_FSDP = X * Y
BF16 = jnp.bfloat16
F32 = jnp.float32


def prepare(
    tokens,
    out_grad,
    routes,
    probs,
    gate_elems,
    gate_scales,
    up_elems,
    up_scales,
    down_elems,
    down_scales,
    payload,
    everyone,
):
    width = tokens.shape[1]
    weights = (
        (gate_elems, gate_scales),
        (up_elems, up_scales),
        (down_elems, down_scales),
    )
    for place, (elements, scales) in enumerate(weights):
        units = elements.shape[1]
        columns = slice(place * units, (place + 1) * units)
        wide = scales[...].astype(F32)
        for group in range(scales.shape[0]):
            rows = slice(group * BLOCK, (group + 1) * BLOCK)
            scaled = (elements[rows, :].astype(F32) * wide[group : group + 1, :]).astype(BF16)
            for receiver in range(everyone.shape[0]):
                everyone[receiver, rows, columns] = scaled
    count = tokens.shape[0]
    named = routes[...] == 0
    chances = probs[...].astype(F32)
    first, second = named[0:1, :], named[1:2, :]
    chosen = jnp.where(jnp.logical_or(first, second), 1.0, 0.0)
    weight = jnp.where(first, chances[0:1, :], jnp.where(second, chances[1:2, :], 0.0))
    down = lax.broadcasted_iota(jnp.int32, (count, count), 0)
    across = lax.broadcasted_iota(jnp.int32, (count, count), 1)

    def column(mask, row):
        return jnp.sum(jnp.where(mask, row, 0.0), axis=1, keepdims=True)

    chosen_column = column(down == across, chosen)
    weight_column = column(down == across, weight)
    place_column = column(across <= down, chosen)
    wide_weight = jnp.broadcast_to(weight_column, (count, 128))
    parts = (tokens[...].astype(F32), out_grad[...].astype(F32), wide_weight)
    starts = (0, width, 2 * width)
    for start, part in zip(starts, parts):
        picked = []
        for slot in range(CAP):
            here = jnp.where(place_column == slot + 1.0, chosen_column, 0.0)
            picked.append(jnp.sum(here * part, axis=0, keepdims=True))
        block = jnp.concatenate(picked, axis=0).astype(BF16)
        payload[:, start : start + part.shape[1]] = block


def local(
    tokens,
    out_grad,
    routes,
    probs,
    gate_elems,
    gate_scales,
    up_elems,
    up_scales,
    down_elems,
    down_scales,
):
    width = tokens.shape[1]
    units = gate_elems.shape[1]
    own_shape = (gate_elems.shape[0], 3 * units)
    payload, everyone = pl.pallas_call(
        prepare,
        out_shape=(
            jax.ShapeDtypeStruct((CAP, 2 * width + 128), BF16),
            jax.ShapeDtypeStruct((N_FSDP,) + own_shape, BF16),
        ),
        compiler_params=pltpu.CompilerParams(vmem_limit_bytes=60 * 1024 * 1024),
    )(
        tokens,
        out_grad,
        routes.T,
        probs.T,
        gate_elems,
        gate_scales,
        up_elems,
        up_scales,
        down_elems.T,
        down_scales.T,
    )
    weights = lax.all_to_all(everyone, ("x", "y"), 0, 0, tiled=True)

    along_z = lax.all_gather(payload[None], ("za", "zb", "zc"), axis=0, tiled=True)
    along_z = along_z.reshape(2 * FAR * CAP, payload.shape[1])
    along_z = lax.all_gather(along_z, "zd", axis=0, tiled=True)
    along_z, weights = lax.optimization_barrier((along_z, weights))
    pair = jnp.broadcast_to(along_z[None], (CORES,) + along_z.shape)
    pair = lax.all_to_all(pair, "core", 0, 0, tiled=True)
    all_rows = pair.reshape(CORES * FAR * NEAR * CAP, payload.shape[1])
    rows = all_rows[:, :width]
    grads_rows = all_rows[:, width : 2 * width]
    row_weights = all_rows[:, 2 * width : 2 * width + 1].astype(F32)

    weights = weights.reshape(N_FSDP * own_shape[0], own_shape[1])
    w_gate, w_up, w_down = (
        weights[:, :units],
        weights[:, units : 2 * units],
        weights[:, 2 * units :],
    )

    gate_pre = jnp.dot(rows, w_gate, preferred_element_type=F32)
    lift_pre = jnp.dot(rows, w_up, preferred_element_type=F32)
    back = jnp.dot(grads_rows, w_down, preferred_element_type=F32)
    sigmoid_gate = jax.nn.sigmoid(gate_pre)
    activated = gate_pre * sigmoid_gate
    hidden = (activated * lift_pre).astype(BF16)
    scaled_hidden = (row_weights * activated * lift_pre).astype(BF16)
    prob_part = jnp.sum(hidden.astype(F32) * back, axis=1, keepdims=True)
    hidden_grad = row_weights * back
    lift_grad = (hidden_grad * activated).astype(BF16)
    gate_pre_grad = (
        hidden_grad * lift_pre * sigmoid_gate * (1.0 + gate_pre * (1.0 - sigmoid_gate))
    ).astype(BF16)

    def over_rows(a, b):
        return lax.dot_general(a, b, (((0,), (0,)), ((), ())), preferred_element_type=F32)

    terms = jnp.concatenate(
        [
            over_rows(rows, gate_pre_grad),
            over_rows(rows, lift_grad),
            over_rows(grads_rows, scaled_hidden),
        ],
        axis=1,
    ).astype(BF16)
    terms = terms.reshape((N_FSDP,) + own_shape)
    input_part = lax.dot_general(
        jnp.concatenate([gate_pre_grad, lift_grad], axis=1),
        weights[:, : 2 * units],
        (((1,), (1,)), ((), ())),
        preferred_element_type=F32,
    )

    def pack(values, prob):
        high = prob.astype(BF16)
        low = (prob - high.astype(F32)).astype(BF16)
        pad = jnp.zeros(prob.shape[:-1] + (126,), BF16)
        return jnp.concatenate([values.astype(BF16), high, low, pad], axis=-1)

    def unpack(blocks):
        total = jnp.sum(blocks.astype(F32), axis=0)
        prob = total[..., width : width + 1] + total[..., width + 1 : width + 2]
        return total[..., :width], prob

    part = pack(input_part, prob_part).reshape(CORES, FAR * NEAR * CAP, -1)
    part = lax.all_to_all(part, "core", 0, 0, tiled=True)
    part = pack(*unpack(part)).reshape(2, FAR, 2, CAP, -1)
    part = part.transpose(2, 0, 1, 3, 4).reshape(NEAR, FAR * CAP, -1)
    part = lax.all_to_all(part, NEAR_AXES, 0, 0, tiled=True)
    part = pack(*unpack(part))
    part, terms = lax.optimization_barrier((part, terms))
    shares = lax.all_to_all(terms, ("x", "y"), 0, 0, tiled=True)
    share = jnp.sum(shares.astype(F32), axis=0)

    def halve(part, axis, where):
        bit = lax.axis_index(axis)
        keep = lax.dynamic_index_in_dim(part, bit, where, keepdims=False)
        give = lax.dynamic_index_in_dim(part, 1 - bit, where, keepdims=False)
        return pack(*unpack(jnp.stack([keep, lax.ppermute(give, axis, SWAP)])))

    part = halve(part.reshape(4, 2, CAP, -1), "zb", 1).reshape(4 * CAP, -1)
    part = lax.all_gather(part[None], "za", axis=0, tiled=True)
    mine = CAP * lax.axis_index("za")
    input_rows, prob_rows = unpack(lax.dynamic_slice_in_dim(part, mine, CAP, axis=1))

    chosen = jnp.any(routes == 0, axis=1)
    slot = jnp.cumsum(chosen.astype(jnp.int32)) - 1
    slot_ids = jnp.arange(CAP, dtype=jnp.int32)
    select_mask = jnp.logical_and(slot[None, :] == slot_ids[:, None], chosen[None, :])
    mask_float = select_mask.astype(F32)
    input_grad = jnp.sum(
        mask_float[:, :, None] * input_rows.astype(BF16).astype(F32)[:, None, :], axis=0
    ).astype(BF16)
    prob_grad = jnp.sum(mask_float * prob_rows, axis=0)
    gate_grad = share[:, :units]
    up_grad = share[:, units : 2 * units]
    down_grad = share[:, 2 * units :].T
    return (input_grad, prob_grad, gate_grad, up_grad, down_grad)


def solution(mesh):
    fine = Mesh(
        mesh.devices.reshape(4, 2, 2, 2, CORES, X, Y),
        FAR_AXES + NEAR_AXES + ("core", "x", "y"),
    )
    ep, fsdp = FAR_AXES + NEAR_AXES + ("core",), ("x", "y")
    by_token = P(ep + fsdp, None)
    tall, wide = P(fsdp, ep), P(ep, fsdp)
    in_specs = (by_token,) * 4 + (tall,) * 4 + (wide,) * 2
    out_specs = (by_token, P(ep + fsdp), tall, tall, wide)
    return jax.shard_map(
        local, mesh=fine, in_specs=in_specs, out_specs=out_specs, check_vma=False
    )
```
